256 devices in a mesh: row: 16 (over x, z_lo, core), col: 4 (over z_hi), aux: 4 (over y).
Axes of the slice: x: 4, y: 4, z: 8 (z_hi: 4, z_lo: 2; z = z_hi * 2 + z_lo), core: 2. Of those that a mesh axis runs over, the one named last changes fastest.
Arguments:
- colloc: bfloat16 [4096, 4096], P(('row', 'col'), 'aux'), may hold values from -6 to 6
- coulomb: bfloat16 [4096, 16384], P(('row', 'col'), 'aux'), may hold values from -6 to 6
- geminal: bfloat16 [4096, 20480], P(('row', 'col'), 'aux'), may hold values from -6 to 6
- occupied: bfloat16 [4096, 256], P(('row', 'col')), may hold values from -6 to 6
Outputs:
- pair_field: float32 [4096, 256], P(('row', 'col', 'aux'))
- energy: float32 [256], replicated
The draws below stay inside these ranges and needn't reach their ends.
All inputs are finite; a program needn't handle non-finite values.
Results may differ from the reference program's by a relative error of at most 0.0057.
Values may be sent and summed in bfloat16 or wider, within the bound.
No kernel may reach another device: no remote copies, remote signals or barrier semaphores. Data moves between devices by JAX's collectives and lax.ppermute only.
A program may use at most 128 MiB of HBM per device.

```python
import math
import jax
import jax.numpy as jnp
from jax import lax

NBAS = 4096
NAUXC = 16384
NAUXF = 20480
NOCC = 256
NGRID = 4096


def shard_levels(stream_key, dims, pieces, low, largest):
    level = 1.0
    for position, parts in pieces:
        heights = jax.random.uniform(jax.random.fold_in(jax.random.fold_in(stream_key, 6), position), (parts,), jnp.float32, low / len(pieces), largest / len(pieces))
        level = level * jnp.repeat(jnp.exp(heights), dims[position] // parts).reshape((-1,) + (1,) * (len(dims) - 1 - position))
    return level


def gaussian(key, dims, scale, bound, shards=(), kind=jnp.bfloat16):
    factor_of = shard_levels(key, dims, shards, -0.22, 0.18) if shards else 1.0
    entries = jax.random.normal(key, dims, jnp.float32) * scale * factor_of
    return jnp.minimum(jnp.maximum(entries, -bound), bound).astype(kind)


def setup_inputs(seed: int = 0) -> dict:
    key_of = jax.random.split(jax.random.key(seed), 5)
    return {
        "colloc": gaussian(key_of[0], (NGRID, NBAS), 1.0, 6.0, ((0, 64), (1, 4))),
        "coulomb": gaussian(key_of[1], (NGRID, NAUXC), 1.0, 6.0, ((0, 64), (1, 4))),
        "geminal": gaussian(key_of[2], (NGRID, NAUXF), 1.0, 6.0, ((0, 64), (1, 4))),
        "occupied": gaussian(key_of[3], (NGRID, NOCC), 1.0, 6.0, ((0, 64),)),
    }


def reference(colloc, coulomb, geminal, occupied):
    basis_gram = jnp.dot(colloc, colloc.T, preferred_element_type=jnp.float32) / math.sqrt(NBAS)
    coul_fit = jnp.dot(coulomb, coulomb.T, preferred_element_type=jnp.float32) / math.sqrt(NAUXC)
    gem_fit = jnp.dot(geminal, geminal.T, preferred_element_type=jnp.float32) / math.sqrt(NAUXF)
    index = jnp.arange(NGRID, dtype=jnp.int32)
    same = index[:, None] == index[None, :]
    kernel = jnp.where(same, jnp.float32(0.0), basis_gram * basis_gram * coul_fit * gem_fit).astype(jnp.bfloat16)
    occ_float = occupied.astype(jnp.float32)
    occ_weight = (occ_float * occ_float).astype(jnp.bfloat16)
    pair_field = jnp.dot(kernel, occ_weight, preferred_element_type=jnp.float32) / math.sqrt(NGRID)
    weight_back = lax.optimization_barrier(occ_weight).astype(jnp.float32)
    energy = lax.optimization_barrier(jnp.sum(weight_back * pair_field, axis=0)) / math.sqrt(NGRID)
    return (pair_field, energy)
```

```python
import math

import jax
import jax.numpy as jnp
from jax import lax
from jax.sharding import Mesh, PartitionSpec as P

NBAS = 4096
NAUXC = 16384
NAUXF = 20480
NGRID = 4096
ZN = 8
YN = 4


def z_slot(z):
    return (z % 2) * (ZN // 2) + z // 2


def shift_z(v, d):
    return lax.ppermute(v, ("l", "h"), [(z_slot(z), z_slot((z + d) % ZN)) for z in range(ZN)])


def shift_x(v, d):
    return lax.ppermute(v, "x", [(i, (i + d) % 4) for i in range(4)])


def swap_core(v):
    return lax.ppermute(v, "c", [(0, 1), (1, 0)])


def shards(colloc, coulomb, geminal, occupied):
    points = colloc.shape[0]
    sub = points // YN
    core = lax.axis_index("c")
    xi = lax.axis_index("x")
    yi = lax.axis_index("y")
    z = lax.axis_index("h") * 2 + lax.axis_index("l")

    full = jnp.stack([geminal, jnp.concatenate([coulomb, colloc], axis=1)])

    occ_z = lax.all_gather(occupied, ("l", "h"), axis=0, tiled=False)
    own_occ = lax.dynamic_slice_in_dim(occupied, yi * sub, sub, 0)
    occ_x = lax.all_gather(own_occ, ("x", "c"), axis=0, tiled=True).astype(jnp.float32)
    w_row = (occ_x * occ_x).astype(jnp.bfloat16)

    xf1, xb1 = shift_x(full, 1), shift_x(full, -1)
    f1, b1 = shift_z(full, 1), shift_z(full, -1)
    x2g, x2c = shift_x(xf1[0], 1), shift_x(xb1[1], -1)
    f2, b2 = shift_z(f1, 1), shift_z(b1, -1)
    f3, b3 = shift_z(f2, 1), shift_z(b2, -1)
    f4, b4 = shift_z(f3[0], 1), shift_z(b3[1], -1)

    o0, of1, ob1 = swap_core(full), swap_core(xf1), swap_core(xb1)
    o2g, o2c = swap_core(x2g), swap_core(x2c)

    def rows(blocks):
        return jnp.concatenate([b.reshape(YN, sub, b.shape[-1]) for b in blocks], axis=1)

    row_g = rows([full[0], o0[0], xb1[0], ob1[0], x2g, o2g, xf1[0], of1[0]])
    row_c = rows([full[1], o0[1], xb1[1], ob1[1], x2c, o2c, xf1[1], of1[1]])

    def gram(cg, cc):
        t = jnp.stack(
            [
                jnp.einsum("qk,ypk->yqp", cg, row_g, preferred_element_type=jnp.float32),
                jnp.einsum("qk,ypk->yqp", cc[:, :NAUXC // YN], row_c[:, :, : NAUXC // YN], preferred_element_type=jnp.float32),
                jnp.einsum("qk,ypk->yqp", cc[:, NAUXC // YN :], row_c[:, :, NAUXC // YN :], preferred_element_type=jnp.float32),
            ],
            axis=1,
        )
        s = lax.all_to_all(t, "y", 0, 0, tiled=True).sum(0)
        bas = s[2] / math.sqrt(NBAS)
        return bas * bas * (s[1] / math.sqrt(NAUXC)) * (s[0] / math.sqrt(NAUXF))

    def pair(a, b):
        return jnp.concatenate([a[0], b[0]]), jnp.concatenate([a[1], b[1]])

    k0 = gram(full[0], full[1])
    q = lax.broadcasted_iota(jnp.int32, k0.shape, 0)
    p = lax.broadcasted_iota(jnp.int32, k0.shape, 1)
    k0 = jnp.where((p < sub) & (q == p + yi * sub), jnp.float32(0.0), k0)
    k1 = gram(*pair(f1, b1))
    k2 = gram(*pair(f2, b2))
    k3 = gram(*pair(f3, b3))
    k4 = gram(f4, b4)
    kern = jnp.concatenate([k0, k1, k2, k3, k4], axis=0).astype(jnp.bfloat16)

    order = jnp.array([0, -1, 1, -2, 2, -3, 3, 4], jnp.int32) + z
    order = order % ZN
    occ_c = jnp.take(occ_z, (order % 2) * (ZN // 2) + order // 2, axis=0).astype(jnp.float32)
    w_col = (occ_c * occ_c).astype(jnp.bfloat16).reshape(ZN * points, -1)

    part = lax.dot_general(
        kern, w_col, (((0,), (0,)), ((), ())), preferred_element_type=jnp.float32
    ) / math.sqrt(NGRID)
    part = part.reshape(4, 2, sub, -1)
    gx = (jnp.arange(4, dtype=jnp.int32) - xi) % 4
    part = jnp.take(part, gx, axis=0)
    part = jnp.where(core == 0, part, part[:, ::-1])
    part = part.reshape(8, sub, -1)
    local = jnp.sum(
        w_row.astype(jnp.float32).reshape(8 * sub, -1) * part.reshape(8 * sub, -1), axis=0
    ) / math.sqrt(NGRID)
    send = jnp.concatenate([part, jnp.broadcast_to(local, (8, 8, local.shape[0]))], axis=1)
    got = lax.all_to_all(send, ("x", "c"), 0, 0, tiled=True)
    pair_field = got[:, :sub].sum(0)
    energy = got[:, sub].sum(0)
    energy = lax.all_to_all(
        jnp.broadcast_to(energy, (32, 1, energy.shape[0])), ("l", "h", "y"), 0, 0, tiled=True
    ).sum((0, 1))
    return pair_field, energy


def solution(mesh):
    fine = Mesh(mesh.devices.reshape(4, 2, 2, 4, 4), ("x", "l", "c", "h", "y"))
    grid = ("x", "l", "c", "h")
    in_specs = (P(grid, "y"), P(grid, "y"), P(grid, "y"), P(grid, None))
    out_specs = (P(grid + ("y",), None), P())
    return jax.shard_map(shards, mesh=fine, in_specs=in_specs, out_specs=out_specs, check_vma=False)
```

```python
import math

import jax
import jax.numpy as jnp
from jax import lax
from jax.sharding import Mesh, PartitionSpec as P

NBAS = 4096
NAUXC = 16384
NAUXF = 20480
NGRID = 4096
ZN = 8
YN = 4


def z_slot(z):
    return (z % 2) * (ZN // 2) + z // 2


def shift_z(v, d):
    return lax.ppermute(v, ("l", "h"), [(z_slot(z), z_slot((z + d) % ZN)) for z in range(ZN)])


def shift_x(v, d):
    return lax.ppermute(v, "x", [(i, (i + d) % 4) for i in range(4)])


def swap_core(v):
    return lax.ppermute(v, "c", [(0, 1), (1, 0)])


def spread(v, axes, count):
    return lax.all_to_all(jnp.broadcast_to(v, (count,) + v.shape), axes, 0, 0, tiled=True)


def shards(colloc, coulomb, geminal, occupied):
    points = colloc.shape[0]
    sub = points // YN
    core = lax.axis_index("c")
    xi = lax.axis_index("x")
    yi = lax.axis_index("y")
    z = lax.axis_index("h") * 2 + lax.axis_index("l")

    full = jnp.stack([geminal, jnp.concatenate([coulomb, colloc], axis=1)])

    occ_z = spread(occupied, ("l", "h"), ZN)
    own_occ = lax.dynamic_slice_in_dim(occupied, yi * sub, sub, 0)
    occ_x = spread(own_occ, ("x", "c"), 8).astype(jnp.float32)
    w_row = (occ_x * occ_x).astype(jnp.bfloat16)

    xf1, xb1 = shift_x(full, 1), shift_x(full, -1)
    f1, b1 = shift_z(full, 1), shift_z(full, -1)
    x2g, x2c = shift_x(xf1[0], 1), shift_x(xb1[1], -1)
    f2, b2 = shift_z(f1, 1), shift_z(b1, -1)
    f3, b3 = shift_z(f2, 1), shift_z(b2, -1)
    f4, b4 = shift_z(f3[0], 1), shift_z(b3[1], -1)

    o0, of1, ob1 = swap_core(full), swap_core(xf1), swap_core(xb1)
    o2g, o2c = swap_core(x2g), swap_core(x2c)

    def rows(blocks):
        return jnp.concatenate([b.reshape(YN, sub, b.shape[-1]) for b in blocks], axis=1)

    row_g = rows([full[0], o0[0], xb1[0], ob1[0], x2g, o2g, xf1[0], of1[0]])
    row_c = rows([full[1], o0[1], xb1[1], ob1[1], x2c, o2c, xf1[1], of1[1]])

    def gram(cg, cc):
        t = jnp.stack(
            [
                jnp.einsum("qk,ypk->yqp", cg, row_g, preferred_element_type=jnp.float32),
                jnp.einsum("qk,ypk->yqp", cc[:, :NAUXC // YN], row_c[:, :, : NAUXC // YN], preferred_element_type=jnp.float32),
                jnp.einsum("qk,ypk->yqp", cc[:, NAUXC // YN :], row_c[:, :, NAUXC // YN :], preferred_element_type=jnp.float32),
            ],
            axis=1,
        )
        s = lax.all_to_all(t, "y", 0, 0, tiled=True).sum(0)
        bas = s[2] / math.sqrt(NBAS)
        return bas * bas * (s[1] / math.sqrt(NAUXC)) * (s[0] / math.sqrt(NAUXF))

    def pair(a, b):
        return jnp.concatenate([a[0], b[0]]), jnp.concatenate([a[1], b[1]])

    k0 = gram(full[0], full[1])
    q = lax.broadcasted_iota(jnp.int32, k0.shape, 0)
    p = lax.broadcasted_iota(jnp.int32, k0.shape, 1)
    k0 = jnp.where((p < sub) & (q == p + yi * sub), jnp.float32(0.0), k0)
    k1 = gram(*pair(f1, b1))
    k2 = gram(*pair(f2, b2))
    k3 = gram(*pair(f3, b3))
    k4 = gram(f4, b4)
    kern = jnp.concatenate([k0, k1, k2, k3, k4], axis=0).astype(jnp.bfloat16)

    order = jnp.array([0, -1, 1, -2, 2, -3, 3, 4], jnp.int32) + z
    order = order % ZN
    occ_c = jnp.take(occ_z, (order % 2) * (ZN // 2) + order // 2, axis=0).astype(jnp.float32)
    w_col = (occ_c * occ_c).astype(jnp.bfloat16).reshape(ZN * points, -1)

    part = lax.dot_general(
        kern, w_col, (((0,), (0,)), ((), ())), preferred_element_type=jnp.float32
    ) / math.sqrt(NGRID)
    part = part.reshape(4, 2, sub, -1)
    gx = (jnp.arange(4, dtype=jnp.int32) - xi) % 4
    part = jnp.take(part, gx, axis=0)
    part = jnp.where(core == 0, part, part[:, ::-1])
    part = part.reshape(8, sub, -1)
    local = jnp.sum(
        w_row.astype(jnp.float32).reshape(8 * sub, -1) * part.reshape(8 * sub, -1), axis=0
    ) / math.sqrt(NGRID)
    send = jnp.concatenate([part, jnp.broadcast_to(local, (8, 8, local.shape[0]))], axis=1)
    got = lax.all_to_all(send, ("x", "c"), 0, 0, tiled=True)
    pair_field = got[:, :sub].sum(0)
    energy = got[:, sub].sum(0)
    energy = lax.all_to_all(
        jnp.broadcast_to(energy, (32, 1, energy.shape[0])), ("l", "h", "y"), 0, 0, tiled=True
    ).sum((0, 1))
    return pair_field, energy


def solution(mesh):
    fine = Mesh(mesh.devices.reshape(4, 2, 2, 4, 4), ("x", "l", "c", "h", "y"))
    grid = ("x", "l", "c", "h")
    in_specs = (P(grid, "y"), P(grid, "y"), P(grid, "y"), P(grid, None))
    out_specs = (P(grid + ("y",), None), P())
    return jax.shard_map(shards, mesh=fine, in_specs=in_specs, out_specs=out_specs, check_vma=False)
```

```python
import functools
import math

import jax
import jax.numpy as jnp
from jax import lax
from jax.experimental import pallas as pl
from jax.experimental.pallas import tpu as pltpu
from jax.sharding import Mesh, PartitionSpec as P

NBAS = 4096
NAUXC = 16384
NAUXF = 20480
NGRID = 4096
ZN = 8
XN = 4
YN = 4
LANES = 128
GROUP = 4
SCALES = (math.sqrt(NAUXF), math.sqrt(NAUXC), math.sqrt(NBAS))
VMEM = pl.BlockSpec(memory_space=pltpu.VMEM)
SMEM = pl.BlockSpec(memory_space=pltpu.SMEM)


def tie(*values):
    return lax.optimization_barrier(values)


def z_slot(z):
    return (z % 2) * (ZN // 2) + z // 2


def shift_z(v, d):
    return lax.ppermute(v, ("l", "h"), [(z_slot(z), z_slot((z + d) % ZN)) for z in range(ZN)])


def shift_x(v, d):
    return lax.ppermute(v, "x", [(i, (i + d) % XN) for i in range(XN)])


def swap_core(v):
    return lax.ppermute(v, "c", [(0, 1), (1, 0)])


def spread(v, axes, count):
    return lax.all_to_all(jnp.broadcast_to(v, (count,) + v.shape), axes, 0, 0, tiled=True)


def over_y(t):
    return lax.all_to_all(t, "y", 0, 0, tiled=True)


def squared(v):
    v = v.astype(jnp.float32)
    return (v * v).astype(jnp.bfloat16)


def call(body, out, args):
    several = isinstance(out, tuple)
    return pl.pallas_call(
        body,
        out_shape=out,
        in_specs=[SMEM] + [VMEM] * (len(args) - 1),
        out_specs=tuple(VMEM for _ in out) if several else VMEM,
        cost_estimate=pl.CostEstimate(flops=0, bytes_accessed=0, transcendentals=0),
        compiler_params=pltpu.CompilerParams(vmem_limit_bytes=32 * 1024 * 1024),
    )(*args)


def pack_body(place, *refs):
    parts, (kept, given) = refs[:-2], refs[-2:]
    core = place[0]
    slab = 0
    for ref in parts:
        half = ref.shape[1] // 2
        for i in range(half // LANES):
            for out, which in ((kept, core), (given, 1 - core)):
                start = pl.multiple_of(which * half + i * LANES, LANES)
                out[slab] = ref[:, pl.ds(start, LANES)]
            slab += 1


def merge_body(place, kept, got, occ, out):
    core = place[0]
    n, points, _ = kept.shape
    out[:n, pl.ds(pl.multiple_of(core * points, points), points)] = kept[...]
    out[:n, pl.ds(pl.multiple_of((1 - core) * points, points), points)] = got[...]
    out[n, :points] = occ[:, :LANES]
    out[n, points:] = occ[:, LANES:]


def tile_body(cuts, sizes, place, *refs):
    blocks = []
    for n in sizes:
        blocks.append(refs[:n])
        refs = refs[n:]
    keep, *send = refs

    def slab(block, t):
        first = block[0].shape[0]
        return block[0][t] if len(block) == 1 or t < first else block[1][t - first]

    rows, cols = blocks[:XN], blocks[XN:]
    points = keep.shape[2] // len(cols)
    sub = points // YN
    core = place[0]
    for j, (a, b) in enumerate(zip(cuts, cuts[1:])):
        acc = None
        for s in range(a, b, GROUP):
            r, q = [], []
            for t in range(s, s + GROUP):
                slabs = [slab(x, t) for x in rows]
                r.append(
                    jnp.concatenate(
                        [
                            x[c * points + y * sub : c * points + (y + 1) * sub]
                            for y in range(YN)
                            for x in slabs
                            for c in range(2)
                        ]
                    )
                )
                q.append(jnp.concatenate([slab(x, t) for x in cols]))
            part = lax.dot_general(
                jnp.concatenate(q, axis=1),
                jnp.concatenate(r, axis=1),
                (((1,), (1,)), ((), ())),
                preferred_element_type=jnp.float32,
            )
            acc = part if acc is None else acc + part
        width = 2 * points
        for n in range(len(cols)):
            first = acc[2 * n * points : (2 * n + 1) * points]
            second = acc[(2 * n + 1) * points : (2 * n + 2) * points]
            to, at = (send[0], j) if len(send) == 1 else (send[j], 0)
            for out, i, t in (
                (keep, j, jnp.where(core == 0, first, second)),
                (to, at, jnp.where(core == 0, second, first)),
            ):
                for y in range(YN):
                    out[y, i, n * points : (n + 1) * points] = t[:, y * width : (y + 1) * width]


def tiles(cuts, place, rows, cols, split=False):
    points = rows[0][0].shape[1] // 2
    blocks = tuple(rows) + tuple(cols)

    def out(n):
        return jax.ShapeDtypeStruct((YN, n, len(cols) * points, 2 * points), jnp.float32)

    outs = (out(3),) + ((out(1),) * 3 if split else (out(3),))
    body = functools.partial(tile_body, cuts, tuple(len(b) for b in blocks))
    return call(body, outs, (place,) + tuple(ref for b in blocks for ref in b))


def add_body(place, a, *refs):
    *others, out = refs
    if len(others) == 1:
        out[...] = a[...] + others[0][...]
    else:
        for j, other in enumerate(others):
            out[:, j] = a[:, j] + other[:, 0]


def add(place, a, *others):
    return call(add_body, jax.ShapeDtypeStruct(a.shape, a.dtype), (place, a) + others)


def orbitals_body(place, *refs):
    for i, ref in enumerate(refs[:-1]):
        refs[-1][i] = ref[0]


def orbitals(place, blocks):
    n, width = len(blocks), blocks[0].shape[1:]

    def last(b):
        at = b.shape[0] - 1
        return pl.BlockSpec((1,) + width, lambda i: (at, 0, 0))

    return pl.pallas_call(
        orbitals_body,
        out_shape=jax.ShapeDtypeStruct((n,) + width, blocks[0].dtype),
        grid=(1,),
        in_specs=[SMEM] + [last(b) for b in blocks],
        out_specs=pl.BlockSpec((n,) + width, lambda i: (0, 0, 0)),
        cost_estimate=pl.CostEstimate(flops=0, bytes_accessed=0, transcendentals=0),
    )(place, *blocks)


def field(place, s, cols, diagonal):
    t = s[0] + s[1] + s[2] + s[3]
    bas = t[2] / SCALES[2]
    kern = bas * bas * (t[1] / SCALES[1]) * (t[0] / SCALES[0])
    points = cols[0].shape[1] // 2
    sub = points // YN
    if diagonal:
        q = lax.broadcasted_iota(jnp.int32, kern.shape, 0)
        p = lax.broadcasted_iota(jnp.int32, kern.shape, 1) - place[0] * sub
        kern = jnp.where((p >= 0) & (p < sub) & (q == p + place[1] * sub), jnp.float32(0.0), kern)
    last = [c[c.shape[0] - 1] for c in cols]
    w = squared(jnp.concatenate([jnp.concatenate([c[:points], c[points:]], axis=1) for c in last]))
    return lax.dot_general(
        kern.astype(jnp.bfloat16), w, (((0,), (0,)), ((), ())), preferred_element_type=jnp.float32
    )


def apply_body(diagonal, place, s, *refs):
    refs[-1][...] = field(place, s, refs[:-1], diagonal)


def apply(place, s, cols, diagonal=False):
    out = jax.ShapeDtypeStruct((s.shape[-1], 2 * LANES), jnp.float32)
    return call(functools.partial(apply_body, diagonal), out, (place, s) + tuple(cols))


def last_body(place, s, col, p1, p2, p3, own, other, out):
    part = (field(place, s, [col], False) + p1[...] + p2[...] + p3[...]) / math.sqrt(NGRID)
    core, y, x = place[0], place[1], place[2]
    points = own.shape[1] // 2
    sub = points // YN
    energy = jnp.zeros((sub, part.shape[1]), jnp.float32)
    at = pl.multiple_of(y * sub, sub)
    for i in range(XN):
        for c in range(2):
            w = jnp.concatenate(
                [
                    jnp.where(core == c, own[i, pl.ds(o + at, sub)], other[i, pl.ds(o + at, sub)])
                    for o in (0, points)
                ],
                axis=1,
            )
            mine = part[(2 * i + c) * sub : (2 * i + c + 1) * sub]
            energy += squared(w).astype(jnp.float32) * mine
            out[2 * ((i + x) % XN) + c, :sub] = mine
    total = jnp.sum(energy, axis=0, keepdims=True) / math.sqrt(NGRID)
    for g in range(2 * XN):
        out[g, sub:] = jnp.broadcast_to(total, (8, total.shape[1]))


def shards(colloc, coulomb, geminal, occupied):
    points = colloc.shape[0]
    sub = points // YN
    place = jnp.stack([lax.axis_index("c"), lax.axis_index("y"), lax.axis_index("x")]).astype(jnp.int32)

    n_slabs = (geminal.shape[1] + coulomb.shape[1] + colloc.shape[1]) // (2 * LANES)
    half = geminal.shape[1] // (2 * LANES)
    cuts = (0, half, half + coulomb.shape[1] // (2 * LANES), n_slabs)
    piece = jax.ShapeDtypeStruct((n_slabs, points, LANES), jnp.bfloat16)
    kept, given = call(pack_body, (piece, piece), (place, geminal, coulomb, colloc))
    block = call(
        merge_body,
        jax.ShapeDtypeStruct((n_slabs + 1, 2 * points, LANES), jnp.bfloat16),
        (place, kept, swap_core(given), occupied),
    )

    f1, b1 = shift_z(block, 1), shift_z(block, -1)
    xf1, xb1 = shift_x(block, 1), shift_x(block, -1)
    f1, b1, xf1, xb1 = tie(f1, b1, xf1, xb1)

    f2, b2 = shift_z(f1, 1), shift_z(b1, -1)
    x2a, x2b = shift_x(xf1[:half], 1), shift_x(xb1[half:], -1)
    rows = ((block,), (xb1,), (x2a, x2b), (xf1,))
    keep, send = tiles(cuts, place, rows, ((block,), (f1,), (b1,)))
    t1 = add(place, keep, swap_core(send))
    f2, b2, t1 = tie(f2, b2, t1)

    f3, b3 = shift_z(f2, 1), shift_z(b2, -1)
    s1 = over_y(t1)
    keep, send = tiles(cuts, place, rows, ((f2,), (b2,)))
    t2 = add(place, keep, swap_core(send))
    own = orbitals(place, (block, xb1, x2b, xf1))
    other = swap_core(own)
    f3, b3, s1, t2, other = tie(f3, b3, s1, t2, other)

    f4, b4 = shift_z(f3[:half], 1), shift_z(b3[half:], -1)
    s2 = over_y(t2)
    keep, *send = tiles(cuts, place, rows, ((f3,), (b3,)), split=True)
    t3 = add(place, keep, *[swap_core(v) for v in send])
    p1 = apply(place, s1, (block, f1, b1), diagonal=True)
    f4, b4, s2, t3, p1 = tie(f4, b4, s2, t3, p1)

    s3 = over_y(t3)
    keep, send = tiles(cuts, place, rows, ((f4, b4),))
    s4 = over_y(add(place, keep, swap_core(send)))
    p2 = apply(place, s2, (f2, b2))
    p3 = apply(place, s3, (f3, b3))
    sent = call(
        last_body,
        jax.ShapeDtypeStruct((2 * XN, sub + 8, 2 * LANES), jnp.float32),
        (place, s4, b4, p1, p2, p3, own, other),
    )
    got = lax.all_to_all(sent, ("x", "c"), 0, 0, tiled=True)
    pair_field = got[:, :sub].sum(0)
    energy = got[:, sub].sum(0)
    energy = spread(energy[None], ("l", "h", "y"), ZN * YN).sum((0, 1))
    return pair_field, energy


def solution(mesh):
    fine = Mesh(mesh.devices.reshape(4, 2, 2, 4, 4), ("x", "l", "c", "h", "y"))
    grid = ("x", "l", "c", "h")
    in_specs = (P(grid, "y"), P(grid, "y"), P(grid, "y"), P(grid, None))
    out_specs = (P(grid + ("y",), None), P())
    return jax.shard_map(shards, mesh=fine, in_specs=in_specs, out_specs=out_specs, check_vma=False)
```

```python
import functools
import math

import jax
import jax.numpy as jnp
from jax import lax
from jax.experimental import pallas as pl
from jax.experimental.pallas import tpu as pltpu
from jax.sharding import Mesh, PartitionSpec as P

NBAS = 4096
NAUXC = 16384
NAUXF = 20480
NGRID = 4096
ZN = 8
XN = 4
YN = 4
LANES = 128
GROUP = 4
SCALES = (math.sqrt(NAUXF), math.sqrt(NAUXC), math.sqrt(NBAS))
VMEM = pl.BlockSpec(memory_space=pltpu.VMEM)
SMEM = pl.BlockSpec(memory_space=pltpu.SMEM)


def tie(*values):
    return lax.optimization_barrier(values)


def z_slot(z):
    return (z % 2) * (ZN // 2) + z // 2


def shift_z(v, d):
    return lax.ppermute(v, ("l", "h"), [(z_slot(z), z_slot((z + d) % ZN)) for z in range(ZN)])


def shift_x(v, d):
    return lax.ppermute(v, "x", [(i, (i + d) % XN) for i in range(XN)])


def swap_core(v):
    return lax.ppermute(v, "c", [(0, 1), (1, 0)])


def spread(v, axes, count):
    return lax.all_to_all(jnp.broadcast_to(v, (count,) + v.shape), axes, 0, 0, tiled=True)


def over_y(t):
    return lax.all_to_all(t, "y", 0, 0, tiled=True)


def squared(v):
    v = v.astype(jnp.float32)
    return (v * v).astype(jnp.bfloat16)


def call(body, out, args):
    several = isinstance(out, tuple)
    return pl.pallas_call(
        body,
        out_shape=out,
        in_specs=[SMEM] + [VMEM] * (len(args) - 1),
        out_specs=tuple(VMEM for _ in out) if several else VMEM,
        cost_estimate=pl.CostEstimate(flops=0, bytes_accessed=0, transcendentals=0),
        compiler_params=pltpu.CompilerParams(vmem_limit_bytes=32 * 1024 * 1024),
    )(*args)


def pack_body(given, place, *refs):
    parts, out = refs[:-1], refs[-1]
    which = 1 - place[0] if given else place[0]
    slab = 0
    for ref in parts:
        width = ref.shape[1] // 2
        for i in range(width // LANES):
            out[slab] = ref[:, pl.ds(pl.multiple_of(which * width + i * LANES, LANES), LANES)]
            slab += 1


def pack(place, parts, given):
    slabs = sum(v.shape[1] for v in parts) // (2 * LANES)
    out = jax.ShapeDtypeStruct((slabs, parts[0].shape[0], LANES), parts[0].dtype)
    return call(functools.partial(pack_body, given), out, (place,) + parts)


def merge_body(place, kept, got, occ, out):
    core = place[0]
    n, points, _ = kept.shape
    out[:n, pl.ds(pl.multiple_of(core * points, points), points)] = kept[...]
    out[:n, pl.ds(pl.multiple_of((1 - core) * points, points), points)] = got[...]
    out[n, :points] = occ[:, :LANES]
    out[n, points:] = occ[:, LANES:]


def halves_body(half, place, a, b, first, second, sems):
    copies = [
        pltpu.make_async_copy(a.at[:half], first, sems.at[0]),
        pltpu.make_async_copy(b.at[half:], second, sems.at[1]),
    ]
    for copy in copies:
        copy.start()
    for copy in copies:
        copy.wait()


def halves(half, place, a, b):
    anywhere = pl.BlockSpec(memory_space=pl.ANY)
    n = a.shape[0]
    return pl.pallas_call(
        functools.partial(halves_body, half),
        out_shape=(
            jax.ShapeDtypeStruct((half,) + a.shape[1:], a.dtype),
            jax.ShapeDtypeStruct((n - half,) + a.shape[1:], a.dtype),
        ),
        in_specs=[SMEM, anywhere, anywhere],
        out_specs=(VMEM, VMEM),
        scratch_shapes=[pltpu.SemaphoreType.DMA((2,))],
        cost_estimate=pl.CostEstimate(flops=0, bytes_accessed=0, transcendentals=0),
        compiler_params=pltpu.CompilerParams(vmem_limit_bytes=32 * 1024 * 1024),
    )(place, a, b)


def tile_body(cuts, sizes, place, *refs):
    blocks = []
    for n in sizes:
        blocks.append(refs[:n])
        refs = refs[n:]
    keep, *send = refs

    def slab(block, t):
        first = block[0].shape[0]
        return block[0][t] if len(block) == 1 or t < first else block[1][t - first]

    rows, cols = blocks[:XN], blocks[XN:]
    points = keep.shape[2] // len(cols)
    sub = points // YN
    core = place[0]
    for j, (a, b) in enumerate(zip(cuts, cuts[1:])):
        acc = None
        for s in range(a, b, GROUP):
            r, q = [], []
            for t in range(s, s + GROUP):
                slabs = [slab(x, t) for x in rows]
                r.append(
                    jnp.concatenate(
                        [
                            x[c * points + y * sub : c * points + (y + 1) * sub]
                            for y in range(YN)
                            for x in slabs
                            for c in range(2)
                        ]
                    )
                )
                q.append(jnp.concatenate([slab(x, t) for x in cols]))
            part = lax.dot_general(
                jnp.concatenate(q, axis=1),
                jnp.concatenate(r, axis=1),
                (((1,), (1,)), ((), ())),
                preferred_element_type=jnp.float32,
            )
            acc = part if acc is None else acc + part
        width = 2 * points
        for n in range(len(cols)):
            first = acc[2 * n * points : (2 * n + 1) * points]
            second = acc[(2 * n + 1) * points : (2 * n + 2) * points]
            to, at = (send[0], j) if len(send) == 1 else (send[j], 0)
            for out, i, t in (
                (keep, j, jnp.where(core == 0, first, second)),
                (to, at, jnp.where(core == 0, second, first)),
            ):
                for y in range(YN):
                    out[y, i, n * points : (n + 1) * points] = t[:, y * width : (y + 1) * width]


def tiles(cuts, place, rows, cols, split=False):
    points = rows[0][0].shape[1] // 2
    blocks = tuple(rows) + tuple(cols)

    def out(n):
        return jax.ShapeDtypeStruct((YN, n, len(cols) * points, 2 * points), jnp.float32)

    outs = (out(3),) + ((out(1),) * 3 if split else (out(3),))
    body = functools.partial(tile_body, cuts, tuple(len(b) for b in blocks))
    return call(body, outs, (place,) + tuple(ref for b in blocks for ref in b))


def add_body(place, a, *refs):
    *others, out = refs
    if len(others) == 1:
        out[...] = a[...] + others[0][...]
    else:
        for j, other in enumerate(others):
            out[:, j] = a[:, j] + other[:, 0]


def add(place, a, *others):
    return call(add_body, jax.ShapeDtypeStruct(a.shape, a.dtype), (place, a) + others)


def call_last(body, out, args, blocks):
    def whole(v):
        zeros = (0,) * len(v.shape)
        return pl.BlockSpec(v.shape, lambda i: zeros)

    def last(b):
        at = b.shape[0] - 1
        return pl.BlockSpec((1,) + b.shape[1:], lambda i: (at, 0, 0))

    return pl.pallas_call(
        body,
        out_shape=out,
        grid=(1,),
        in_specs=[SMEM] + [whole(v) for v in args[1:]] + [last(b) for b in blocks],
        out_specs=whole(out),
        cost_estimate=pl.CostEstimate(flops=0, bytes_accessed=0, transcendentals=0),
        compiler_params=pltpu.CompilerParams(vmem_limit_bytes=32 * 1024 * 1024),
    )(*args, *blocks)


def orbitals_body(place, *refs):
    for i, ref in enumerate(refs[:-1]):
        refs[-1][i] = ref[0]


def orbitals(place, blocks):
    out = jax.ShapeDtypeStruct((len(blocks),) + blocks[0].shape[1:], blocks[0].dtype)
    return call_last(orbitals_body, out, (place,), blocks)


def shift_y(v, d):
    return lax.ppermute(v, "y", [(i, (i + d) % YN) for i in range(YN)])


def add_ring_body(place, a, b, *outs):
    for k, out in enumerate(outs):
        i = (place[1] + k) % YN
        out[...] = a[i] + b[i]


def over_y_ring(place, a, b):
    out = jax.ShapeDtypeStruct(a.shape[1:], a.dtype)
    terms = call(add_ring_body, (out,) * YN, (place, a, b))
    return tuple(shift_y(v, k) if k else v for k, v in enumerate(terms))


def field(place, s, cols, diagonal):
    t = s[0][...] + s[1][...] + s[2][...] + s[3][...]
    bas = t[2] / SCALES[2]
    kern = bas * bas * (t[1] / SCALES[1]) * (t[0] / SCALES[0])
    points = cols[0].shape[1] // 2
    sub = points // YN
    if diagonal:
        q = lax.broadcasted_iota(jnp.int32, kern.shape, 0)
        p = lax.broadcasted_iota(jnp.int32, kern.shape, 1) - place[0] * sub
        kern = jnp.where((p >= 0) & (p < sub) & (q == p + place[1] * sub), jnp.float32(0.0), kern)
    last = [c[0] for c in cols]
    w = squared(jnp.concatenate([jnp.concatenate([c[:points], c[points:]], axis=1) for c in last]))
    return lax.dot_general(
        kern.astype(jnp.bfloat16), w, (((0,), (0,)), ((), ())), preferred_element_type=jnp.float32
    )


def apply_body(diagonal, place, s, *refs):
    refs[-1][...] = field(place, s, refs[:-1], diagonal)


def apply(place, s, cols, diagonal=False):
    out = jax.ShapeDtypeStruct((s.shape[-1], 2 * LANES), jnp.float32)
    return call_last(functools.partial(apply_body, diagonal), out, (place, s), tuple(cols))


def last_body(place, s0, s1, s2, s3, p1, p2, p3, own, other, col, out):
    part = (field(place, (s0, s1, s2, s3), [col], False) + p1[...] + p2[...] + p3[...]) / math.sqrt(NGRID)
    core, y, x = place[0], place[1], place[2]
    points = own.shape[1] // 2
    sub = points // YN
    energy = jnp.zeros((sub, part.shape[1]), jnp.float32)
    at = pl.multiple_of(y * sub, sub)
    for i in range(XN):
        for c in range(2):
            w = jnp.concatenate(
                [
                    jnp.where(core == c, own[i, pl.ds(o + at, sub)], other[i, pl.ds(o + at, sub)])
                    for o in (0, points)
                ],
                axis=1,
            )
            mine = part[(2 * i + c) * sub : (2 * i + c + 1) * sub]
            energy += squared(w).astype(jnp.float32) * mine
            out[2 * ((i + x) % XN) + c, :sub] = mine
    total = jnp.sum(energy, axis=0, keepdims=True) / math.sqrt(NGRID)
    for g in range(2 * XN):
        out[g, sub:] = jnp.broadcast_to(total, (8, total.shape[1]))


def shards(colloc, coulomb, geminal, occupied):
    points = colloc.shape[0]
    sub = points // YN
    place = jnp.stack([lax.axis_index("c"), lax.axis_index("y"), lax.axis_index("x")]).astype(jnp.int32)

    n_slabs = (geminal.shape[1] + coulomb.shape[1] + colloc.shape[1]) // (2 * LANES)
    half = geminal.shape[1] // (2 * LANES)
    cuts = (0, half, half + coulomb.shape[1] // (2 * LANES), n_slabs)
    parts = (geminal, coulomb, colloc)
    given = swap_core(pack(place, parts, True))
    block = call(
        merge_body,
        jax.ShapeDtypeStruct((n_slabs + 1, 2 * points, LANES), jnp.bfloat16),
        (place, pack(place, parts, False), given, occupied),
    )

    f1, b1 = shift_z(block, 1), shift_z(block, -1)
    xf1, xb1 = shift_x(block, 1), shift_x(block, -1)

    f2, b2 = shift_z(f1, 1), shift_z(b1, -1)
    x2a, x2b = shift_x(xf1[:half], 1), shift_x(xb1[half:], -1)
    rows = ((block,), (xb1,), (x2a, x2b), (xf1,))
    keep, send = tiles(cuts, place, rows, ((block,), (f1,), (b1,)))
    t1 = add(place, keep, swap_core(send))
    f2, b2, t1 = tie(f2, b2, t1)

    f3, b3 = shift_z(f2, 1), shift_z(b2, -1)
    s1 = over_y(t1)
    keep, send = tiles(cuts, place, rows, ((f2,), (b2,)))
    t2 = add(place, keep, swap_core(send))
    own = orbitals(place, (block, xb1, x2b, xf1))
    other = swap_core(own)
    f3, b3, s1, t2, other = tie(f3, b3, s1, t2, other)

    f4, b4 = halves(half, place, f3, b3)
    f4, b4 = shift_z(f4, 1), shift_z(b4, -1)
    s2 = over_y(t2)
    keep, *send = tiles(cuts, place, rows, ((f3,), (b3,)), split=True)
    t3 = add(place, keep, *[swap_core(v) for v in send])
    p1 = apply(place, s1, (block, f1, b1), diagonal=True)
    f4, b4, s2, t3, p1 = tie(f4, b4, s2, t3, p1)

    s3 = over_y(t3)
    keep, send = tiles(cuts, place, rows, ((f4, b4),))
    s4 = over_y_ring(place, keep, swap_core(send))
    p2 = apply(place, s2, (f2, b2))
    p3 = apply(place, s3, (f3, b3))
    sent = call_last(
        last_body,
        jax.ShapeDtypeStruct((2 * XN, sub + 8, 2 * LANES), jnp.float32),
        (place,) + s4 + (p1, p2, p3, own, other),
        (b4,),
    )
    got = lax.all_to_all(sent, ("x", "c"), 0, 0, tiled=True)
    pair_field = got[:, :sub].sum(0)
    energy = got[:, sub].sum(0)
    energy = spread(energy[None], ("l", "h", "y"), ZN * YN).sum((0, 1))
    return pair_field, energy


def solution(mesh):
    fine = Mesh(mesh.devices.reshape(4, 2, 2, 4, 4), ("x", "l", "c", "h", "y"))
    grid = ("x", "l", "c", "h")
    in_specs = (P(grid, "y"), P(grid, "y"), P(grid, "y"), P(grid, None))
    out_specs = (P(grid + ("y",), None), P())
    return jax.shard_map(shards, mesh=fine, in_specs=in_specs, out_specs=out_specs, check_vma=False)
```

```python
import functools
import math

import jax
import jax.numpy as jnp
from jax import lax
from jax.experimental import pallas as pl
from jax.experimental.pallas import tpu as pltpu
from jax.sharding import Mesh, PartitionSpec as P

NBAS = 4096
NAUXC = 16384
NAUXF = 20480
NGRID = 4096
ZN = 8
XN = 4
YN = 4
LANES = 128
GROUP = 4
SCALES = (math.sqrt(NAUXF), math.sqrt(NAUXC), math.sqrt(NBAS))
VMEM = pl.BlockSpec(memory_space=pltpu.VMEM)
SMEM = pl.BlockSpec(memory_space=pltpu.SMEM)


def tie(*values):
    return lax.optimization_barrier(values)


def z_slot(z):
    return (z % 2) * (ZN // 2) + z // 2


def shift_z(v, d):
    return lax.ppermute(v, ("l", "h"), [(z_slot(z), z_slot((z + d) % ZN)) for z in range(ZN)])


def shift_x(v, d):
    return lax.ppermute(v, "x", [(i, (i + d) % XN) for i in range(XN)])


def swap_core(v):
    return lax.ppermute(v, "c", [(0, 1), (1, 0)])


def spread(v, axes, count):
    return lax.all_to_all(jnp.broadcast_to(v, (count,) + v.shape), axes, 0, 0, tiled=True)


def over_y(t):
    return lax.all_to_all(t, "y", 0, 0, tiled=True)


def squared(v):
    v = v.astype(jnp.float32)
    return (v * v).astype(jnp.bfloat16)


def call(body, out, args):
    several = isinstance(out, tuple)
    return pl.pallas_call(
        body,
        out_shape=out,
        in_specs=[SMEM] + [VMEM] * (len(args) - 1),
        out_specs=tuple(VMEM for _ in out) if several else VMEM,
        cost_estimate=pl.CostEstimate(flops=0, bytes_accessed=0, transcendentals=0),
        compiler_params=pltpu.CompilerParams(vmem_limit_bytes=32 * 1024 * 1024),
    )(*args)


def pack_body(given, place, *refs):
    parts, out = refs[:-1], refs[-1]
    which = 1 - place[0] if given else place[0]
    slab = 0
    for ref in parts:
        width = ref.shape[1] // 2
        for i in range(width // LANES):
            out[slab] = ref[:, pl.ds(pl.multiple_of(which * width + i * LANES, LANES), LANES)]
            slab += 1


def pack(place, parts, given):
    slabs = sum(v.shape[1] for v in parts) // (2 * LANES)
    out = jax.ShapeDtypeStruct((slabs, parts[0].shape[0], LANES), parts[0].dtype)
    return call(functools.partial(pack_body, given), out, (place,) + parts)


def merge_body(place, kept, got, occ, *outs):
    core = place[0]
    _, points, _ = kept.shape
    start = 0
    for out in outs:
        n = out.shape[0] - 1
        for ref, which in ((kept, core), (got, 1 - core)):
            at = pl.ds(pl.multiple_of(which * points, points), points)
            out[:n, at] = ref[start : start + n]
        out[n, :points] = occ[:, :LANES]
        out[n, points:] = occ[:, LANES:]
        start += n


def fetch_body(cuts, count, place, *refs):
    sources, (keep, send), held, sems = refs[:count], refs[count : count + 2], refs[count + 2 : -1], refs[-1]
    copies = [pltpu.make_async_copy(a, b, sems.at[i]) for i, (a, b) in enumerate(zip(sources, held))]
    n = count // 2 - XN
    kinds = tuple(range(XN)) + tuple(range(2 * XN, 2 * XN + n)), tuple(range(XN, 2 * XN)) + tuple(range(2 * XN + n, count))
    for kind in kinds:
        for i in kind:
            copies[i].start()
    tile_body(cuts, place, *held, keep, send, ready=[[copies[i] for i in kind] for kind in kinds])


def tile_body(cuts, place, *refs, ready=None):
    keep, send = refs[-2:]
    n = (len(refs) - 2) // 2 - XN
    rows, cols = (refs[:XN], refs[XN : 2 * XN]), (refs[2 * XN : 2 * XN + n], refs[2 * XN + n : -2])
    points = keep.shape[2] // n
    core, twist = place[0], 2 * lax.rem(place[2], 2)
    for j, (kind, a, b) in enumerate(cuts):
        if ready and a == 0:
            for copy in ready[kind]:
                copy.wait()
        acc = None
        for s in range(a, b, GROUP):
            group = range(s, s + GROUP)
            r = jnp.concatenate([jnp.concatenate([x[t] for x in rows[kind]]) for t in group], axis=1)
            q = jnp.concatenate([jnp.concatenate([x[t] for x in cols[kind]]) for t in group], axis=1)
            part = lax.dot_general(q, r, (((1,), (1,)), ((), ())), preferred_element_type=jnp.float32)
            acc = part if acc is None else acc + part
        for i in range(n):
            first = acc[2 * i * points : (2 * i + 1) * points]
            second = acc[(2 * i + 1) * points : (2 * i + 2) * points]
            for out, t in (
                (keep, jnp.where(core == 0, first, second)),
                (send, jnp.where(core == 0, second, first)),
            ):
                for e in range(XN):
                    y = lax.rem(e + twist, YN)
                    out[y, j, i * points : (i + 1) * points] = t[:, 2 * e * points : 2 * (e + 1) * points]


def tiles(cuts, place, rows, cols, fetch=False):
    points = rows[0][0].shape[1] // 2
    out = jax.ShapeDtypeStruct((YN, 3, len(cols) * points, 2 * points), jnp.float32)
    args = [b[kind] for blocks in (rows, cols) for kind in range(2) for b in blocks]
    if not fetch:
        return call(functools.partial(tile_body, cuts), (out, out), (place, *args))
    return pl.pallas_call(
        functools.partial(fetch_body, cuts, len(args)),
        out_shape=(out, out),
        in_specs=[SMEM] + [pl.BlockSpec(memory_space=pl.ANY)] * len(args),
        out_specs=(VMEM, VMEM),
        scratch_shapes=[pltpu.VMEM(v.shape, v.dtype) for v in args] + [pltpu.SemaphoreType.DMA((len(args),))],
        cost_estimate=pl.CostEstimate(flops=0, bytes_accessed=0, transcendentals=0),
        compiler_params=pltpu.CompilerParams(vmem_limit_bytes=56 * 1024 * 1024),
    )(place, *args)


def add_body(place, a, b, out):
    out[...] = a[...] + b[...]


def add(place, a, b):
    return call(add_body, jax.ShapeDtypeStruct(a.shape, a.dtype), (place, a, b))


def call_last(body, out, args, blocks):
    def whole(v):
        zeros = (0,) * len(v.shape)
        return pl.BlockSpec(v.shape, lambda i: zeros)

    def last(b):
        at = b.shape[0] - 1
        return pl.BlockSpec((1,) + b.shape[1:], lambda i: (at, 0, 0))

    return pl.pallas_call(
        body,
        out_shape=out,
        grid=(1,),
        in_specs=[SMEM] + [whole(v) for v in args[1:]] + [last(b) for b in blocks],
        out_specs=whole(out),
        cost_estimate=pl.CostEstimate(flops=0, bytes_accessed=0, transcendentals=0),
        compiler_params=pltpu.CompilerParams(vmem_limit_bytes=32 * 1024 * 1024),
    )(*args, *blocks)


def orbitals_body(place, *refs):
    for i, ref in enumerate(refs[:-1]):
        refs[-1][i] = ref[0]


def orbitals(place, blocks):
    out = jax.ShapeDtypeStruct((len(blocks),) + blocks[0].shape[1:], blocks[0].dtype)
    return call_last(orbitals_body, out, (place,), blocks)


def shift_y(v, d):
    return lax.ppermute(v, "y", [(i, (i + d) % YN) for i in range(YN)])


def add_ring_body(place, a, b, *outs):
    for k, out in enumerate(outs):
        i = (place[1] + k) % YN
        out[...] = a[i] + b[i]


def over_y_ring(place, a, b):
    out = jax.ShapeDtypeStruct(a.shape[1:], a.dtype)
    terms = call(add_ring_body, (out,) * YN, (place, a, b))
    return tuple(shift_y(v, k) if k else v for k, v in enumerate(terms))


def shift_pair(v, d):
    pairs = []
    for x in range(XN):
        for z in range(ZN):
            for y in range(YN):
                to = (y - x) % XN
                source = (x * ZN + z_slot(z)) * YN + y
                pairs.append((source, (to * ZN + z_slot((z + d) % ZN)) * YN + y))
    return lax.ppermute(v, ("x", "l", "h", "y"), pairs)


def geminal_and_rest(t):
    bas = t[2] / SCALES[2]
    return t[0] / SCALES[0], bas * bas * (t[1] / SCALES[1])


def turn_body(place, s, zero, own_g, own_r, *outs):
    core = place[0]
    t = s[0] + s[1] + s[2] + s[3]
    g, r = geminal_and_rest(t)
    points = g.shape[1] // 2
    steps = g.shape[0] // points - 1
    zero[0] = g[:points]
    zero[1] = r[:points]
    own_g[...] = g[points:]
    own_r[...] = r[points:]
    mine, give = outs
    for kind, v in enumerate((g, r)):
        for i in range(steps):
            turned = v[(i + 1) * points : (i + 2) * points].T
            lo, hi = turned[:points], turned[points:]
            mine[kind * steps + i] = jnp.where(core == 0, lo, hi)
            give[kind * steps + i] = jnp.where(core == 0, hi, lo)


def turn(place, s):
    rows, lanes = s.shape[2:]
    points = lanes // 2
    steps = rows // points - 1

    def f32(*shape):
        return jax.ShapeDtypeStruct(shape, jnp.float32)

    outs = (f32(2, points, lanes),) + (f32(rows - points, lanes),) * 2 + (f32(2 * steps, points, points),) * 2
    return call(turn_body, outs, (place, s))


def join_body(place, mine, got, *outs):
    core = place[0]
    for i, out in enumerate(outs):
        a, b = mine[i], got[i]
        out[...] = jnp.concatenate([jnp.where(core == 0, a, b), jnp.where(core == 0, b, a)], axis=1)


def join(place, mine, got):
    n, points, _ = mine.shape
    return call(join_body, (jax.ShapeDtypeStruct((points, 2 * points), jnp.float32),) * n, (place, mine, got))


def last_body(steps, place, zero, own_g, own_r, *refs):
    far, others = refs[:YN], refs[YN : YN + 2 * steps]
    own, other, cols, out = refs[YN + 2 * steps :]
    core, y, x = place[0], place[1], place[2]
    points = zero.shape[1]
    sub = points // YN
    e = lax.rem(y + 2 * lax.rem(x, 2), XN)
    k0 = zero[0] * zero[1]
    q = lax.broadcasted_iota(jnp.int32, k0.shape, 0)
    p = lax.broadcasted_iota(jnp.int32, k0.shape, 1) - core * points
    k0 = jnp.where((e == 0) & (p == q), jnp.float32(0.0), k0)
    g4, r4 = geminal_and_rest(far[0][...] + far[1][...] + far[2][...] + far[3][...])
    kerns = [k0, g4 * r4]
    for i in range(steps):
        at = slice(i * points, (i + 1) * points)
        kerns.append(own_g[at] * others[steps + i][...])
        kerns.append(others[i][...] * own_r[at])
    slabs = [cols[i] for i in range(cols.shape[0])]
    w = squared(jnp.concatenate([jnp.concatenate([c[:points], c[points:]], axis=1) for c in slabs]))
    part = lax.dot_general(
        jnp.concatenate(kerns).astype(jnp.bfloat16), w, (((0,), (0,)), ((), ())), preferred_element_type=jnp.float32
    ) / math.sqrt(NGRID)
    a, b = own[e], other[e]
    w_row = []
    for c in range(2):
        v = jnp.where(core == c, a, b)
        w_row.append(jnp.concatenate([v[:points], v[points:]], axis=1))
    w_row = squared(jnp.concatenate(w_row)).astype(jnp.float32)
    total = jnp.sum(w_row * part, axis=0, keepdims=True) / math.sqrt(NGRID)
    for i in range(2 * YN):
        out[i, :sub] = part[i * sub : (i + 1) * sub]
        out[i, sub:] = jnp.broadcast_to(total, (out.shape[1] - sub, total.shape[1]))


def shards(colloc, coulomb, geminal, occupied):
    points = colloc.shape[0]
    sub = points // YN
    place = jnp.stack([lax.axis_index("c"), lax.axis_index("y"), lax.axis_index("x")]).astype(jnp.int32)

    n_gem = geminal.shape[1] // (2 * LANES)
    n_coul = coulomb.shape[1] // (2 * LANES)
    n_rest = n_coul + colloc.shape[1] // (2 * LANES)
    cuts = ((0, 0, n_gem), (1, 0, n_coul), (1, n_coul, n_rest))
    parts = (geminal, coulomb, colloc)
    given = swap_core(pack(place, parts, True))
    gem, rest = call(
        merge_body,
        tuple(jax.ShapeDtypeStruct((n + 1, 2 * points, LANES), jnp.bfloat16) for n in (n_gem, n_rest)),
        (place, pack(place, parts, False), given, occupied),
    )

    g1, r1 = shift_z(gem, 1), shift_z(rest, -1)
    xfg, xbr = shift_x(gem, 1), shift_x(rest, -1)
    g1, r1, xfg, xbr = tie(g1, r1, xfg, xbr)
    g2, r2 = shift_z(g1, 1), shift_z(r1, -1)
    xfr, xbg = shift_x(rest, 1), shift_x(gem, -1)
    g2, r2, xfr, xbg = tie(g2, r2, xfr, xbg)
    g3, r3 = shift_z(g2, 1), shift_z(r2, -1)
    x2g, x2r = shift_x(xfg, 1), shift_x(xbr, -1)
    g3, r3, x2g, x2r = tie(g3, r3, x2g, x2r)
    rows = ((gem, rest), (xbg, xbr), (x2g, x2r), (xfg, xfr))

    g4, r4 = shift_z(g3, 1), shift_z(r3, -1)
    keep, send = tiles(cuts, place, rows, ((gem, rest), (g1, r1), (g2, r2), (g3, r3)))
    t = add(place, keep, swap_core(send))
    own = orbitals(place, tuple(b[0] for b in rows))
    other = swap_core(own)
    s = over_y(t)

    keep, send = tiles(cuts, place, rows, ((g4, r4),), fetch=True)
    far = over_y_ring(place, keep, swap_core(send))

    orbs = orbitals(place, (gem, g4, g1, r1, g2, r2, g3, r3))
    s, far, orbs, own, other = tie(s, far, orbs, own, other)

    zero, own_g, own_r, mine, give = turn(place, s)
    joined = join(place, mine, swap_core(give))
    steps = len(joined) // 2
    others = [shift_pair(joined[i], -(i + 1)) for i in range(steps)]
    others += [shift_pair(joined[steps + i], i + 1) for i in range(steps)]
    sent = call(
        functools.partial(last_body, steps),
        jax.ShapeDtypeStruct((2 * YN, sub + 8, 2 * LANES), jnp.float32),
        (place, zero, own_g, own_r) + far + tuple(others) + (own, other, orbs),
    )
    sent = lax.ppermute(
        sent, ("x", "y"), [(x * YN + y, (y - x) % XN * YN + y) for x in range(XN) for y in range(YN)]
    )
    got = lax.all_to_all(sent, ("c", "y"), 0, 0, tiled=True)
    pair_field = got[:, :sub].sum(0)
    energy = got[:, sub].sum(0)
    energy = spread(energy[None], ("x", "l", "h"), XN * ZN).sum((0, 1))
    return pair_field, energy


def solution(mesh):
    fine = Mesh(mesh.devices.reshape(4, 2, 2, 4, 4), ("x", "l", "c", "h", "y"))
    grid = ("x", "l", "c", "h")
    in_specs = (P(grid, "y"), P(grid, "y"), P(grid, "y"), P(grid, None))
    out_specs = (P(grid + ("y",), None), P())
    return jax.shard_map(shards, mesh=fine, in_specs=in_specs, out_specs=out_specs, check_vma=False)
```

```python
import functools
import math

import jax
import jax.numpy as jnp
from jax import lax
from jax.experimental import pallas as pl
from jax.experimental.pallas import tpu as pltpu
from jax.sharding import Mesh, PartitionSpec as P

NBAS = 4096
NAUXC = 16384
NAUXF = 20480
NGRID = 4096
ZN = 8
XN = 4
YN = 4
LANES = 128
GROUP = 4
SCALES = (math.sqrt(NAUXF), math.sqrt(NAUXC), math.sqrt(NBAS))
VMEM = pl.BlockSpec(memory_space=pltpu.VMEM)
SMEM = pl.BlockSpec(memory_space=pltpu.SMEM)


def tie(*values):
    return lax.optimization_barrier(values)


def z_slot(z):
    return (z % 2) * (ZN // 2) + z // 2


def shift_z(v, d):
    return lax.ppermute(v, ("l", "h"), [(z_slot(z), z_slot((z + d) % ZN)) for z in range(ZN)])


def shift_x(v, d):
    return lax.ppermute(v, "x", [(i, (i + d) % XN) for i in range(XN)])


def swap_core(v):
    return lax.ppermute(v, "c", [(0, 1), (1, 0)])


def spread(v, axes, count):
    return lax.all_to_all(jnp.broadcast_to(v, (count,) + v.shape), axes, 0, 0, tiled=True)


def over_y(t):
    return lax.all_to_all(t, "y", 0, 0, tiled=True)


def squared(v):
    v = v.astype(jnp.float32)
    return (v * v).astype(jnp.bfloat16)


def call(body, out, args):
    several = isinstance(out, tuple)
    return pl.pallas_call(
        body,
        out_shape=out,
        in_specs=[SMEM] + [VMEM] * (len(args) - 1),
        out_specs=tuple(VMEM for _ in out) if several else VMEM,
        cost_estimate=pl.CostEstimate(flops=0, bytes_accessed=0, transcendentals=0),
        compiler_params=pltpu.CompilerParams(vmem_limit_bytes=32 * 1024 * 1024),
    )(*args)


def pack_body(given, place, *refs):
    parts, out = refs[:-1], refs[-1]
    which = 1 - place[0] if given else place[0]
    slab = 0
    for ref in parts:
        width = ref.shape[1] // 2
        for i in range(width // LANES):
            out[slab] = ref[:, pl.ds(pl.multiple_of(which * width + i * LANES, LANES), LANES)]
            slab += 1


def pack(place, parts, given):
    slabs = sum(v.shape[1] for v in parts) // (2 * LANES)
    out = jax.ShapeDtypeStruct((slabs, parts[0].shape[0], LANES), parts[0].dtype)
    return call(functools.partial(pack_body, given), out, (place,) + parts)


def merge_body(place, kept, got, occ, *outs):
    core = place[0]
    _, points, _ = kept.shape
    start = 0
    for out in outs:
        n = out.shape[0] - 1
        for ref, which in ((kept, core), (got, 1 - core)):
            at = pl.ds(pl.multiple_of(which * points, points), points)
            out[:n, at] = ref[start : start + n]
        out[n, :points] = occ[:, :LANES]
        out[n, points:] = occ[:, LANES:]
        start += n


def fetch_body(cuts, count, place, *refs):
    sources, (keep, send), held, sems = refs[:count], refs[count : count + 2], refs[count + 2 : -1], refs[-1]
    copies = [pltpu.make_async_copy(a, b, sems.at[i]) for i, (a, b) in enumerate(zip(sources, held))]
    n = count // 2 - XN
    kinds = tuple(range(XN)) + tuple(range(2 * XN, 2 * XN + n)), tuple(range(XN, 2 * XN)) + tuple(range(2 * XN + n, count))
    for kind in kinds:
        for i in kind:
            copies[i].start()
    tile_body(cuts, place, *held, keep, send, ready=[[copies[i] for i in kind] for kind in kinds])


def tile_body(cuts, place, *refs, ready=None):
    keep, send = refs[-2:]
    n = (len(refs) - 2) // 2 - XN
    rows, cols = (refs[:XN], refs[XN : 2 * XN]), (refs[2 * XN : 2 * XN + n], refs[2 * XN + n : -2])
    points = keep.shape[2] // n
    core, twist = place[0], 2 * lax.rem(place[2], 2)
    for j, (kind, a, b) in enumerate(cuts):
        if ready and a == 0:
            for copy in ready[kind]:
                copy.wait()
        acc = None
        for s in range(a, b, GROUP):
            group = range(s, s + GROUP)
            r = jnp.concatenate([jnp.concatenate([x[t] for x in rows[kind]]) for t in group], axis=1)
            q = jnp.concatenate([jnp.concatenate([x[t] for x in cols[kind]]) for t in group], axis=1)
            part = lax.dot_general(q, r, (((1,), (1,)), ((), ())), preferred_element_type=jnp.float32)
            acc = part if acc is None else acc + part
        for i in range(n):
            first = acc[2 * i * points : (2 * i + 1) * points]
            second = acc[(2 * i + 1) * points : (2 * i + 2) * points]
            for out, t in (
                (keep, jnp.where(core == 0, first, second)),
                (send, jnp.where(core == 0, second, first)),
            ):
                for e in range(XN):
                    y = lax.rem(e + twist, YN)
                    out[y, j, i * points : (i + 1) * points] = t[:, 2 * e * points : 2 * (e + 1) * points]


def tiles(cuts, place, rows, cols, fetch=False):
    points = rows[0][0].shape[1] // 2
    out = jax.ShapeDtypeStruct((YN, 3, len(cols) * points, 2 * points), jnp.float32)
    args = [b[kind] for blocks in (rows, cols) for kind in range(2) for b in blocks]
    if not fetch:
        return call(functools.partial(tile_body, cuts), (out, out), (place, *args))
    return pl.pallas_call(
        functools.partial(fetch_body, cuts, len(args)),
        out_shape=(out, out),
        in_specs=[SMEM] + [pl.BlockSpec(memory_space=pl.ANY)] * len(args),
        out_specs=(VMEM, VMEM),
        scratch_shapes=[pltpu.VMEM(v.shape, v.dtype) for v in args] + [pltpu.SemaphoreType.DMA((len(args),))],
        cost_estimate=pl.CostEstimate(flops=0, bytes_accessed=0, transcendentals=0),
        compiler_params=pltpu.CompilerParams(vmem_limit_bytes=56 * 1024 * 1024),
    )(place, *args)


def near_body(place, a, b, near, zero):
    points = zero.shape[2]
    zero[...] = a[:, :, :points] + b[:, :, :points]
    near[...] = a[:, :, points:] + b[:, :, points:]


def rest_body(place, zero, a, b, out):
    points = zero.shape[2]
    out[:, :, :points] = zero[...]
    out[:, :, points:] = a[...] + b[...]


def call_last(body, out, args, blocks):
    def whole(v):
        zeros = (0,) * len(v.shape)
        return pl.BlockSpec(v.shape, lambda i: zeros)

    def last(b):
        at = b.shape[0] - 1
        return pl.BlockSpec((1,) + b.shape[1:], lambda i: (at, 0, 0))

    return pl.pallas_call(
        body,
        out_shape=out,
        grid=(1,),
        in_specs=[SMEM] + [whole(v) for v in args[1:]] + [last(b) for b in blocks],
        out_specs=whole(out),
        cost_estimate=pl.CostEstimate(flops=0, bytes_accessed=0, transcendentals=0),
        compiler_params=pltpu.CompilerParams(vmem_limit_bytes=32 * 1024 * 1024),
    )(*args, *blocks)


def orbitals_body(place, *refs):
    for i, ref in enumerate(refs[:-1]):
        refs[-1][i] = ref[0]


def orbitals(place, blocks):
    out = jax.ShapeDtypeStruct((len(blocks),) + blocks[0].shape[1:], blocks[0].dtype)
    return call_last(orbitals_body, out, (place,), blocks)


def shift_pair(v, d):
    pairs = []
    for x in range(XN):
        for z in range(ZN):
            for y in range(YN):
                to = (y - x) % XN
                source = (x * ZN + z_slot(z)) * YN + y
                pairs.append((source, (to * ZN + z_slot((z + d) % ZN)) * YN + y))
    return lax.ppermute(v, ("x", "l", "h", "y"), pairs)


def geminal_and_rest(t):
    bas = t[2] / SCALES[2]
    return t[0] / SCALES[0], bas * bas * (t[1] / SCALES[1])


def turn_body(place, s, own_g, own_r, *outs):
    core = place[0]
    t = s[0] + s[1] + s[2] + s[3]
    g, r = geminal_and_rest(t)
    points = g.shape[1] // 2
    steps = g.shape[0] // points
    own_g[...] = g
    own_r[...] = r
    mine, give = outs
    for kind, v in enumerate((g, r)):
        for i in range(steps):
            turned = v[i * points : (i + 1) * points].T
            lo, hi = turned[:points], turned[points:]
            mine[kind * steps + i] = jnp.where(core == 0, lo, hi)
            give[kind * steps + i] = jnp.where(core == 0, hi, lo)


def turn(place, s):
    rows, lanes = s.shape[2:]
    points = lanes // 2
    steps = rows // points

    def f32(*shape):
        return jax.ShapeDtypeStruct(shape, jnp.float32)

    outs = (f32(rows, lanes),) * 2 + (f32(2 * steps, points, points),) * 2
    return call(turn_body, outs, (place, s))


def join_body(place, mine, got, *outs):
    core = place[0]
    for i, out in enumerate(outs):
        a, b = mine[i], got[i]
        out[...] = jnp.concatenate([jnp.where(core == 0, a, b), jnp.where(core == 0, b, a)], axis=1)


def join(place, mine, got):
    n, points, _ = mine.shape
    return call(join_body, (jax.ShapeDtypeStruct((points, 2 * points), jnp.float32),) * n, (place, mine, got))


def last_body(steps, place, s, own_g, own_r, *refs):
    others = refs[: 2 * steps]
    own, other, cols, out = refs[2 * steps :]
    core, y, x = place[0], place[1], place[2]
    points = own.shape[1] // 2
    sub = points // YN
    e = lax.rem(y + 2 * lax.rem(x, 2), XN)
    g, r = geminal_and_rest(s[0] + s[1] + s[2] + s[3])
    k0 = g[:points] * r[:points]
    q = lax.broadcasted_iota(jnp.int32, k0.shape, 0)
    p = lax.broadcasted_iota(jnp.int32, k0.shape, 1) - core * points
    k0 = jnp.where((e == 0) & (p == q), jnp.float32(0.0), k0)
    kerns = [k0, g[points:] * r[points:]]
    for i in range(steps):
        at = slice(i * points, (i + 1) * points)
        kerns.append(own_g[at] * others[steps + i][...])
        kerns.append(others[i][...] * own_r[at])
    slabs = [cols[i] for i in range(cols.shape[0])]
    w = squared(jnp.concatenate([jnp.concatenate([c[:points], c[points:]], axis=1) for c in slabs]))
    part = lax.dot_general(
        jnp.concatenate(kerns).astype(jnp.bfloat16), w, (((0,), (0,)), ((), ())), preferred_element_type=jnp.float32
    ) / math.sqrt(NGRID)
    a, b = own[e], other[e]
    w_row = []
    for c in range(2):
        v = jnp.where(core == c, a, b)
        w_row.append(jnp.concatenate([v[:points], v[points:]], axis=1))
    w_row = squared(jnp.concatenate(w_row)).astype(jnp.float32)
    total = jnp.sum(w_row * part, axis=0, keepdims=True) / math.sqrt(NGRID)
    to = lax.rem(y - x + XN, XN)
    out[:, :sub] = jnp.zeros_like(out[:, :sub])
    for i in range(out.shape[0]):
        out[i, sub:] = jnp.broadcast_to(total, (out.shape[1] - sub, total.shape[1]))
    for i in range(2 * YN):
        out[to * 2 * YN + i, :sub] = part[i * sub : (i + 1) * sub]


def shards(colloc, coulomb, geminal, occupied):
    points = colloc.shape[0]
    sub = points // YN
    place = jnp.stack([lax.axis_index("c"), lax.axis_index("y"), lax.axis_index("x")]).astype(jnp.int32)

    n_gem = geminal.shape[1] // (2 * LANES)
    n_coul = coulomb.shape[1] // (2 * LANES)
    n_rest = n_coul + colloc.shape[1] // (2 * LANES)
    cuts = ((0, 0, n_gem), (1, 0, n_coul), (1, n_coul, n_rest))
    parts = (geminal, coulomb, colloc)
    given = swap_core(pack(place, parts, True))
    gem, rest = call(
        merge_body,
        tuple(jax.ShapeDtypeStruct((n + 1, 2 * points, LANES), jnp.bfloat16) for n in (n_gem, n_rest)),
        (place, pack(place, parts, False), given, occupied),
    )

    g1, r1 = shift_z(gem, 1), shift_z(rest, -1)
    xfg, xbr = shift_x(gem, 1), shift_x(rest, -1)
    g1, r1, xfg, xbr = tie(g1, r1, xfg, xbr)
    g2, r2 = shift_z(g1, 1), shift_z(r1, -1)
    xfr, xbg = shift_x(rest, 1), shift_x(gem, -1)
    g2, r2, xfr, xbg = tie(g2, r2, xfr, xbg)
    g3, r3 = shift_z(g2, 1), shift_z(r2, -1)
    x2g, x2r = shift_x(xfg, 1), shift_x(xbr, -1)
    g3, r3, x2g, x2r = tie(g3, r3, x2g, x2r)
    rows = ((gem, rest), (xbg, xbr), (x2g, x2r), (xfg, xfr))

    g4, r4 = shift_z(g3, 1), shift_z(r3, -1)
    keep, send = tiles(cuts, place, rows, ((gem, rest), (g1, r1), (g2, r2), (g3, r3)))
    y, n, _, lanes = keep.shape

    def terms(steps):
        return jax.ShapeDtypeStruct((y, n, steps * points, lanes), jnp.float32)

    near, zero = call(near_body, (terms(3), terms(1)), (place, keep, swap_core(send)))
    own = orbitals(place, tuple(b[0] for b in rows))
    other = swap_core(own)
    s = over_y(near)

    keep, send = tiles(cuts, place, rows, ((g4, r4),), fetch=True)
    rest_terms = call(rest_body, terms(2), (place, zero, keep, swap_core(send)))

    orbs = orbitals(place, (gem, g4, g1, r1, g2, r2, g3, r3))
    s, rest_terms, orbs, own, other = tie(s, rest_terms, orbs, own, other)
    rest = over_y(rest_terms)

    own_g, own_r, mine, give = turn(place, s)
    joined = join(place, mine, swap_core(give))
    steps = len(joined) // 2
    others = [shift_pair(joined[i], -(i + 1)) for i in range(steps)]
    others += [shift_pair(joined[steps + i], i + 1) for i in range(steps)]
    sent = call(
        functools.partial(last_body, steps),
        jax.ShapeDtypeStruct((2 * XN * YN, sub + 8, 2 * LANES), jnp.float32),
        (place, rest, own_g, own_r) + tuple(others) + (own, other, orbs),
    )
    got = lax.all_to_all(sent, ("x", "c", "y"), 0, 0, tiled=True)
    pair_field = got[:, :sub].sum(0)
    energy = got[:, sub].sum(0)
    energy = spread(energy[None], ("l", "h"), ZN).sum((0, 1))
    return pair_field, energy


def solution(mesh):
    fine = Mesh(mesh.devices.reshape(4, 2, 2, 4, 4), ("x", "l", "c", "h", "y"))
    grid = ("x", "l", "c", "h")
    in_specs = (P(grid, "y"), P(grid, "y"), P(grid, "y"), P(grid, None))
    out_specs = (P(grid + ("y",), None), P())
    return jax.shard_map(shards, mesh=fine, in_specs=in_specs, out_specs=out_specs, check_vma=False)
```
